128 devices in a mesh: docs: 128 (over y, x, z, core).
Axes of the slice: x: 4, y: 4, z: 4, core: 2. Of those that a mesh axis runs over, the one named last changes fastest.
Arguments:
- embeddings: bfloat16 [131072, 1024], P('docs'), may hold values from -6 to 6
- cluster_sizes: int32 [64], replicated, may hold values from 1 to 8192, 131072 in all
Outputs:
- row_best: float32 [131072], P('docs')
- cluster_max: float32 [64], replicated
The draws below stay inside these ranges and needn't reach their ends.
Inputs may be any that keep to these rules, and one draw needn't show every extreme that they name: `cluster_sizes`: rows of one cluster are consecutive in the sorted order; the sizes add up to 131072 and the largest is exactly 8192.
All inputs are finite; a program needn't handle non-finite values.
Results may differ from the reference program's by a relative error of at most 0.0013.
Values may be sent and summed in bfloat16 or wider, within the bound.
No kernel may reach another device: no remote copies, remote signals or barrier semaphores. Data moves between devices by JAX's collectives and lax.ppermute only.
A program may use at most 128 MiB of HBM per device.

```python
import math
import jax
import jax.numpy as jnp
import numpy as np
from jax import lax

D = 1024
ROW_DEV = 1024
MOST = 8192
ROWS = 131072
CLUSTERS = 64


def levels(rng, shape, split, least, top_value):
    loudness = 1.0
    for position, shards_of in split:
        draws = jax.random.uniform(jax.random.fold_in(jax.random.fold_in(rng, 6), position), (shards_of,), jnp.float32, least / len(split), top_value / len(split))
        loudness = loudness * jnp.repeat(jnp.exp(draws), shape[position] // shards_of).reshape((-1,) + (1,) * (len(shape) - 1 - position))
    return loudness


def split_up(number_of, total, reach, lean):
    portions = [(1 << 20) // math.isqrt(grade ** lean) + 1 for grade in range(2, number_of + 1)]
    spare, given = total - reach - (number_of - 1), [1] * (number_of - 1)
    while spare > 0:
        movable = [i for i in range(number_of - 1) if given[i] < reach]
        whole, budget = sum([portions[i] for i in movable]), spare
        for i in movable:
            more = min(reach - given[i], max(1, budget * portions[i] // whole), spare)
            given[i] = given[i] + more
            spare = spare - more
    return np.array([reach] + given)


def uneven(stream_key, number_of, total, bound, skew):
    if number_of == 2:
        one = jax.random.randint(stream_key, (), max(1, total - bound), min(bound, total - 1) + 1)
        return jnp.stack([one, total - one])
    tallies = jnp.asarray(split_up(number_of, total, bound, skew), jnp.int32)
    couples = (number_of - 1) // 2
    donor, receiver = tallies[1:1 + 2 * couples:2], tallies[2:2 + 2 * couples:2]
    margin = jnp.minimum(donor - 1, bound - receiver)
    passed = jax.random.randint(jax.random.fold_in(stream_key, 1), (couples,), 0, 1 << 20) % (margin + 1)
    tallies = tallies.at[1:1 + 2 * couples:2].set(donor - passed).at[2:2 + 2 * couples:2].set(receiver + passed)
    return tallies[jax.random.permutation(jax.random.fold_in(stream_key, 2), number_of)]


def normal_values(stream_key, extent, spread, limit, split=(), held_as=jnp.bfloat16):
    level = levels(stream_key, extent, split, -0.22, 0.18) if split else 1.0
    drawn = jax.random.normal(stream_key, extent, jnp.float32) * spread * level
    return jnp.minimum(jnp.maximum(drawn, -limit), limit).astype(held_as)


def setup_inputs(seed: int = 0) -> dict:
    keys = jax.random.split(jax.random.key(seed), 3)
    return {
        "embeddings": normal_values(keys[0], (ROWS, D), 1.0, 6.0, ((0, 128),)),
        "cluster_sizes": uneven(keys[1], CLUSTERS, ROWS, MOST, 2).astype(jnp.int32),
    }


floor_value = -1e+30

def reference(embeddings, cluster_sizes):
    values = embeddings.astype(jnp.float32)
    normed = (values * lax.rsqrt(lax.optimization_barrier(jnp.mean(values * values, axis=1, keepdims=True)) + 1e-06)).astype(jnp.bfloat16)
    normed = lax.optimization_barrier(normed).astype(jnp.float32)
    cluster_ids = jnp.repeat(jnp.arange(CLUSTERS, dtype=jnp.int32), cluster_sizes, total_repeat_length=ROWS)
    positions = jnp.arange(ROWS, dtype=jnp.int32)
    tile_rows = min(256, ROW_DEV)
    tile_count = ROWS // tile_rows
    reach_tiles = MOST // tile_rows + 1
    sim_scale = 1.0 / D
    tile_blocks = normed.reshape(tile_count, tile_rows, D)
    id_blocks = cluster_ids.reshape(tile_count, tile_rows)
    pos_blocks = positions.reshape(tile_count, tile_rows)

    def tile_best(tile_number):
        left_block = tile_blocks[tile_number]
        left_ids = id_blocks[tile_number]
        left_pos = pos_blocks[tile_number]
        best_here = jnp.full((tile_rows,), floor_value, jnp.float32)

        def compute_tile(operands):
            right_block, right_ids, right_pos = operands
            scores = jnp.dot(left_block, right_block.T, precision=lax.Precision.HIGHEST) * sim_scale
            same_cluster = (left_ids[:, None] == right_ids[None, :]) & (left_pos[:, None] != right_pos[None, :])
            return lax.optimization_barrier(jnp.max(jnp.where(same_cluster, scores, floor_value), axis=1))

        def skip_tile(operands):
            return jnp.full((tile_rows,), floor_value, jnp.float32)
        for offset in range(-reach_tiles, reach_tiles + 1):
            partner_tile = tile_number + offset
            inside = (partner_tile >= 0) & (partner_tile < tile_count)
            clipped = jnp.clip(partner_tile, 0, tile_count - 1)
            right_ids = id_blocks[clipped]
            intersection = inside & (left_ids[0] <= right_ids[tile_rows - 1]) & (right_ids[0] <= left_ids[tile_rows - 1])
            tile_part = lax.cond(intersection, compute_tile, skip_tile, (tile_blocks[clipped], right_ids, pos_blocks[clipped]))
            best_here = jnp.maximum(best_here, tile_part)
        return best_here
    row_best = lax.map(tile_best, jnp.arange(tile_count, dtype=jnp.int32)).reshape(ROWS)
    row_best = jnp.maximum(row_best, 0.0)
    cluster_max = jnp.zeros((CLUSTERS,), jnp.float32).at[cluster_ids].max(row_best)
    return (row_best, cluster_max)
```

```python
import functools

import jax
import jax.numpy as jnp
import numpy as np
from jax import lax
from jax.experimental import pallas as pl
from jax.experimental.pallas import tpu as pltpu
from jax.sharding import PartitionSpec as P

AXIS = "docs"
ROWS = 1024
WIDTH = 1024
RING = 8
SLOTS = 6
PIECE = 128
CHUNKS = (256, 256, 256, 256)

RECEIVED = (
    (2, 6, 8),
    (3, 9, 7),
    (5, -6, 1),
    (-4, 0, -5),
    (6, 11, 13),
    (7, 12, 10),
    (0, -3, 4),
    (1, -1, 14),
)
PASSED = (1, 2, 0, 0, 0, 0, 0, 0)
TILES = (
    ((0, 8), (1, 2), (1, 8), (2, 6), (2, 7), (2, 8), (6, 8), (7, 8)),
    ((0, 3), (0, 6), (1, 3), (1, 9), (3, 6), (3, 7), (3, 9), (6, 9)),
    ((-6, -4), (-6, 1), (-6, 2), (-4, 1), (-4, 3), (1, 5), (2, 5)),
    ((-5, -4), (-5, 0), (-5, 2), (-5, 3), (-4, 0), (-4, 2), (0, 2), (0, 5)),
    ((5, 7), (5, 11), (5, 13), (6, 11), (6, 13), (7, 11), (7, 13), (11, 13)),
    ((4, 12), (5, 6), (5, 10), (5, 12), (6, 10), (6, 12), (7, 10), (7, 12)),
    ((-3, 0), (-3, 1), (0, 4), (0, 7), (1, 4), (1, 7), (4, 6), (4, 7)),
    ((-1, 1), (-1, 6), (-1, 7), (1, 6), (6, 14)),
)


def slot_blocks(kind):
    sibling = kind ^ 1
    return (
        (kind, sibling) + RECEIVED[kind] + (RECEIVED[sibling][PASSED[sibling]],)
    )


def tables():
    blocks = np.array([slot_blocks(k) for k in range(RING)], np.int32)
    own, other = [], []
    for k in range(RING):
        held = slot_blocks(k)
        mine, rest = [], []
        for pair in TILES[k]:
            a, b = sorted(held.index(v) for v in pair)
            if a < 2:
                assert b >= 2
                mine.append((a, b))
            else:
                rest.append((a, b))
        own.append(mine)
        other.append(rest)
    most_own = max(len(v) for v in own)
    most_other = max(len(v) for v in other)

    def pack(lists, most):
        out = np.zeros((RING, 1 + 2 * most), np.int32)
        for k, pairs in enumerate(lists):
            out[k, 0] = len(pairs)
            for i, (a, b) in enumerate(pairs):
                out[k, 1 + 2 * i], out[k, 2 + 2 * i] = a, b
        return out

    return blocks, pack(own, most_own), pack(other, most_other)


BLOCKS, OWN_TILES, OTHER_TILES = tables()


def check_cover():
    seen = set()
    for k in range(RING):
        for a, b in TILES[k]:
            d = abs(a - b)
            assert d <= RING and {a, b} <= set(slot_blocks(k))
            low = min(a, b) % RING
            assert (low, d) not in seen
            seen.add((low, d))
    for low in range(RING):
        for d in range(1, RING + 1):
            assert ((low, d) in seen) != (d == 1 and low % 2 == 0)


check_cover()


def routes(count):
    out = []
    for slot in range(3):
        route = []
        for i in range(count):
            source = i - i % RING + RECEIVED[i % RING][slot]
            route.append((source % count, i))
        out.append(route)
    return out


def norm_kernel(x_ref, out_ref):
    v = x_ref[...].astype(jnp.float32)
    mean = jnp.sum(v * v, axis=1, keepdims=True) * (1.0 / WIDTH)
    out_ref[...] = (v * lax.rsqrt(mean + 1e-06)).astype(jnp.bfloat16)


def normalize(embeddings, first, rows):
    step = first // rows
    return pl.pallas_call(
        norm_kernel,
        out_shape=jax.ShapeDtypeStruct((rows, WIDTH), jnp.bfloat16),
        grid=(1,),
        in_specs=[pl.BlockSpec((rows, WIDTH), lambda i: (step, 0))],
        out_specs=pl.BlockSpec((rows, WIDTH), lambda i: (0, 0)),
    )(embeddings)


def lane_maxima(x):
    width = 64
    while x.shape[0] > 8:
        half = x.shape[0] // 2
        top, bottom = x[:half], x[half:]
        lane = lax.broadcasted_iota(jnp.int32, (half, 128), 1)
        low = (lane & width) == 0
        keep = jnp.where(low, top, bottom)
        give = jnp.where(low, bottom, top)
        if width == 64:
            give = pltpu.roll(give, 64, 1)
        else:
            give = jnp.where(low, pltpu.roll(give, 128 - width, 1), pltpu.roll(give, width, 1))
        x = jnp.maximum(keep, give)
        width //= 2
    return x


class Work:
    def __init__(self, data, idc, idr, seg, accr, accc):
        self.data, self.idc, self.idr, self.seg = data, idc, idr, seg
        self.accr, self.accc = accr, accc

    def span(self, slot, first, rows):
        start = self.seg[slot * 16 + first // PIECE]
        end = self.seg[slot * 16 + 8 + (first + rows) // PIECE - 1]
        return start, end

    def shares(self, a, ra, m, b, cb, n):
        a0, a1 = self.span(a, ra, m)
        b0, b1 = self.span(b, cb, n)
        return (a0 <= b1) & (b0 <= a1)

    def tile(self, a, ra, m, b, cb, n, diagonal=False):
        rows = pl.ds(pl.multiple_of(a * ROWS + ra, PIECE), m)
        cols = pl.ds(pl.multiple_of(b * ROWS + cb, PIECE), n)
        scores = lax.dot_general(
            self.data[rows, :],
            self.data[cols, :],
            (((1,), (1,)), ((), ())),
            preferred_element_type=jnp.float32,
        )
        ids = self.idc[rows, :]
        best = self.accr[rows, :]
        for g in range(n // 128):
            at = pl.ds(pl.multiple_of(cb + g * 128, 128), 128)
            same = ids == self.idr[b, :, at]
            if diagonal:
                row = lax.broadcasted_iota(jnp.int32, (m, 128), 0) + ra
                col = lax.broadcasted_iota(jnp.int32, (m, 128), 1) + (cb + g * 128)
                same = same & (row != col)
            v = jnp.where(same, scores[:, g * 128 : (g + 1) * 128], 0.0)
            best = jnp.maximum(best, v)
            self.accc[b, :, at] = jnp.maximum(
                self.accc[b, :, at], jnp.max(v.reshape(m // 8, 8, 128), axis=0)
            )
        self.accr[rows, :] = best

    def finish(self, r_ref, c_ref):
        for s in range(r_ref.shape[0]):
            r_ref[s] = lane_maxima(self.accr[s * ROWS : (s + 1) * ROWS, :])
            c_ref[s] = jnp.max(self.accc[s], axis=0, keepdims=True)


def own_kernel(core_ref, seg_ref, own_ref, sib_ref, idc_ref, idr_ref, r_ref, c_ref, data, accr, accc):
    accr[...] = jnp.zeros_like(accr)
    accc[...] = jnp.zeros_like(accc)
    data[0:ROWS, :] = own_ref[...]
    data[ROWS:, :] = sib_ref[...]
    work = Work(data, idc_ref, idr_ref, seg_ref, accr, accc)
    size = 512

    def within(i, _):
        ra, cb = lax.div(i, 2) * size, lax.rem(i, 2) * size

        @pl.when(work.shares(0, ra, size, 0, cb, size))
        def _():
            work.tile(0, ra, size, 0, cb, size, diagonal=True)

        return 0

    lax.fori_loop(0, 4, within, 0)
    core = core_ref[0]

    def between(i, _):
        ra, cb = core * size, i * size

        @pl.when(work.shares(core, ra, size, 1 - core, cb, size))
        def _():
            work.tile(core, ra, size, 1 - core, cb, size)

        return 0

    lax.fori_loop(0, 2, between, 0)
    work.finish(r_ref, c_ref)


def step_kernel(step, seg_ref, own_ref_t, other_ref_t, idc_ref, idr_ref, *refs):
    count = step + 1
    arrays = refs[: 2 + 4 * count]
    r_ref, c_ref, data, accr, accc, sems = refs[2 + 4 * count :]
    edges = [0]
    for size in CHUNKS:
        edges.append(edges[-1] + size)
    first, size = edges[step], CHUNKS[step]

    def copies():
        out = []
        for s in range(2):
            out.append(pltpu.make_async_copy(arrays[s], data.at[pl.ds(s * ROWS, ROWS)], sems.at[0]))
        for s in range(4):
            k = step
            out.append(
                pltpu.make_async_copy(
                    arrays[2 + s * count + k],
                    data.at[pl.ds((2 + s) * ROWS + edges[k], CHUNKS[k])],
                    sems.at[0],
                )
            )
        late = []
        for s in range(4):
            for k in range(step):
                late.append(
                    pltpu.make_async_copy(
                        arrays[2 + s * count + k],
                        data.at[pl.ds((2 + s) * ROWS + edges[k], CHUNKS[k])],
                        sems.at[1],
                    )
                )
        return out, late

    soon, late = copies()
    for c in soon + late:
        c.start()
    accr[...] = jnp.zeros_like(accr)
    accc[...] = jnp.zeros_like(accc)
    work = Work(data, idc_ref, idr_ref, seg_ref, accr, accc)
    for c in soon:
        c.wait()

    def own_tile(t, _):
        a, b = own_ref_t[1 + 2 * t], own_ref_t[2 + 2 * t]

        @pl.when(work.shares(a, 0, ROWS, b, first, size))
        def _():
            work.tile(a, 0, ROWS, b, first, size)

        return 0

    lax.fori_loop(0, own_ref_t[0], own_tile, 0)
    for c in late:
        c.wait()

    def other_tile(t, _):
        a, b = other_ref_t[1 + 2 * t], other_ref_t[2 + 2 * t]

        @pl.when(work.shares(a, 0, first + size, b, first, size))
        def _():
            work.tile(a, 0, first + size, b, first, size)

        if first > 0:

            @pl.when(work.shares(a, first, size, b, 0, first))
            def _():
                work.tile(a, first, size, b, 0, first)

        return 0

    lax.fori_loop(0, other_ref_t[0], other_tile, 0)
    work.finish(r_ref, c_ref)


VMEM = pl.BlockSpec(memory_space=pltpu.VMEM)
SMEM = pl.BlockSpec(memory_space=pltpu.SMEM)
HBM = pl.BlockSpec(memory_space=pl.ANY)
PARAMS = pltpu.CompilerParams(vmem_limit_bytes=56 * 2**20)


def outputs(slots):
    return (
        jax.ShapeDtypeStruct((slots, 8, 128), jnp.float32),
        jax.ShapeDtypeStruct((slots, 1, ROWS), jnp.float32),
    )


def scratch(slots):
    return [
        pltpu.VMEM((slots * ROWS, WIDTH), jnp.bfloat16),
        pltpu.VMEM((slots * ROWS, 128), jnp.float32),
        pltpu.VMEM((slots, 8, ROWS), jnp.float32),
    ]


def own_maxima(core, seg, own, sibling, idc, idr):
    return pl.pallas_call(
        own_kernel,
        out_shape=outputs(2),
        in_specs=[SMEM, SMEM, VMEM, VMEM, VMEM, VMEM],
        out_specs=(VMEM, VMEM),
        scratch_shapes=scratch(2),
        compiler_params=PARAMS,
    )(core, seg, own, sibling, idc, idr)


def step_maxima(step, seg, own_tiles, other_tiles, idc, idr, arrays):
    return pl.pallas_call(
        functools.partial(step_kernel, step),
        out_shape=outputs(SLOTS),
        in_specs=[SMEM, SMEM, SMEM, VMEM, VMEM] + [HBM] * len(arrays),
        out_specs=(VMEM, VMEM),
        scratch_shapes=scratch(SLOTS) + [pltpu.SemaphoreType.DMA((2,))],
        compiler_params=PARAMS,
    )(seg, own_tiles, other_tiles, idc, idr, *arrays)


def by_row(r, c):
    return jnp.maximum(jnp.swapaxes(r, 1, 2).reshape(r.shape[0], ROWS), c[:, 0, :])


def local(embeddings, cluster_sizes):
    count = lax.axis_size(AXIS)
    clusters = cluster_sizes.shape[0]
    me = lax.axis_index(AXIS)
    kind = lax.rem(me, RING)
    ring = me - kind

    ends = jnp.cumsum(cluster_sizes)
    blocks = (jnp.asarray(BLOCKS)[kind] + ring) % count
    pos = blocks[:, None] * ROWS + jnp.arange(ROWS, dtype=jnp.int32)[None, :]
    ids = jnp.sum((ends[None, None, :] <= pos[:, :, None]).astype(jnp.int32), axis=2)
    seg = jnp.concatenate([ids[:, ::PIECE], ids[:, PIECE - 1 :: PIECE]], axis=1).reshape(-1)
    idr = ids.astype(jnp.float32)[:, None, :]
    idc = jnp.broadcast_to(ids.astype(jnp.float32).reshape(SLOTS * ROWS, 1), (SLOTS * ROWS, 128))
    own_tiles = jnp.asarray(OWN_TILES)[kind]
    other_tiles = jnp.asarray(OTHER_TILES)[kind]

    swap = [(i, i ^ 1) for i in range(count)]
    ways = routes(count)
    parts = []
    first = 0
    for size in CHUNKS:
        parts.append(normalize(embeddings, first, size))
        first += size
    own = jnp.concatenate(parts, axis=0)
    got = [[lax.ppermute(part, AXIS, way) for way in ways] for part in parts]
    sibling = lax.ppermute(own, AXIS, swap)

    found = []
    r, c = own_maxima(
        lax.rem(me, 2).reshape(1), seg, own, sibling, idc[: 2 * ROWS], idr[:2]
    )
    base = by_row(r, c)
    for step in range(len(CHUNKS)):
        r0, r1, r2 = got[step]
        passed = jnp.where(kind == 0, r1, jnp.where(kind == 1, r2, r0))
        got[step].append(lax.ppermute(passed, AXIS, swap))
        arrays = [own, sibling] + [got[k][s] for s in range(4) for k in range(step + 1)]
        found.append(step_maxima(step, seg, own_tiles, other_tiles, idc, idr, arrays))
    r = functools.reduce(jnp.maximum, [f[0] for f in found])
    c = functools.reduce(jnp.maximum, [f[1] for f in found])
    best = by_row(r, c)
    best = jnp.concatenate([jnp.maximum(best[:2], base), best[2:]], axis=0)

    bins = jnp.arange(clusters, dtype=jnp.int32)
    peaks = jnp.max(jnp.where(ids[None] == bins[:, None, None], best[None], 0.0), axis=(1, 2))
    devices = jnp.arange(count, dtype=jnp.int32)
    to = devices[:, None] == blocks[None, :]
    rows = jnp.max(jnp.where(to[:, :, None], best[None], 0.0), axis=1)
    tail = jnp.broadcast_to(peaks[None, :], (count, clusters))
    pad = jnp.zeros((count, 128 - clusters), jnp.float32)
    sent = jnp.concatenate([rows, tail, pad], axis=1).reshape(count, 9, 128)
    back = lax.all_to_all(sent, AXIS, 0, 0, tiled=True)
    final = jnp.max(back, axis=0) * (1.0 / WIDTH)
    return final[:8].reshape(ROWS), final[8, :clusters]


def solution(mesh):
    placed = (P(AXIS, None), P())
    return jax.shard_map(
        local, mesh=mesh, in_specs=placed, out_specs=(P(AXIS), P()), check_vma=False
    )
```

```python
import functools

import jax
import jax.numpy as jnp
import numpy as np
from jax import lax
from jax.experimental import pallas as pl
from jax.experimental.pallas import tpu as pltpu
from jax.sharding import PartitionSpec as P

AXIS = "docs"
ROWS = 1024
WIDTH = 1024
RING = 8
SLOTS = 6
PIECE = 128
STRIP = 256
CHUNKS = (512, 512)
EDGES = (0, 512, 1024)

RECEIVED = (
    (3, 6, 9),
    (2, 8, 7),
    (-4, 1, -6),
    (5, -5, 0),
    (6, 10, 11),
    (7, 12, 13),
    (0, -1, 14),
    (1, -3, 4),
)
PASSED = (1, 2, 0, 0, 0, 0, 0, 2)
TILES = (
    ((0, 3), (0, 7), (1, 9), (3, 6), (3, 7), (3, 9), (6, 9), (7, 9)),
    ((0, 8), (1, 8), (2, 6), (2, 7), (2, 8), (6, 8)),
    ((-6, -4), (-6, 1), (-6, 2), (-4, 1), (-4, 2), (-4, 3), (1, 2), (1, 3), (1, 5)),
    ((-5, -4), (-5, 0), (-5, 2), (-5, 3), (-4, 0), (0, 2), (0, 5), (2, 5), (3, 5)),
    ((5, 10), (5, 11), (6, 10), (6, 11), (7, 10), (7, 11)),
    ((4, 6), (4, 12), (5, 6), (5, 7), (5, 13), (6, 12), (6, 13), (7, 13)),
    ((-1, 0), (-1, 4), (-1, 6), (-1, 7), (0, 4), (4, 7), (6, 14)),
    ((-3, 0), (-3, 1), (-3, 4), (0, 6), (1, 4), (1, 6), (1, 7)),
)


def slot_blocks(kind):
    sibling = kind ^ 1
    return (
        (kind, sibling) + RECEIVED[kind] + (RECEIVED[sibling][PASSED[sibling]],)
    )


def tables():
    blocks = np.array([slot_blocks(k) for k in range(RING)], np.int32)
    tiles = np.zeros((RING, 3 + 2 * max(len(v) for v in TILES)), np.int32)
    for k in range(RING):
        held = slot_blocks(k)
        pairs = sorted(tuple(sorted(held.index(v) for v in pair)) for pair in TILES[k])
        assert (0, 1) not in pairs
        tiles[k, :3] = [sum(a < e for a, _ in pairs) for e in (1, 2, SLOTS)]
        tiles[k, 3 : 3 + 2 * len(pairs)] = np.array(pairs).reshape(-1)
    return blocks, tiles


BLOCKS, KIND_TILES = tables()


def check_cover():
    seen = set()
    for k in range(RING):
        for a, b in TILES[k]:
            d = abs(a - b)
            assert d <= RING and {a, b} <= set(slot_blocks(k))
            low = min(a, b) % RING
            assert (low, d) not in seen
            seen.add((low, d))
    for low in range(RING):
        for d in range(1, RING + 1):
            assert ((low, d) in seen) != (d == 1 and low % 2 == 0)


check_cover()


def routes(count):
    out = []
    for slot in range(3):
        route = []
        for i in range(count):
            source = i - i % RING + RECEIVED[i % RING][slot]
            route.append((source % count, i))
        out.append(route)
    return out


def unit_rows(v):
    v = v.astype(jnp.float32)
    mean = jnp.sum(v * v, axis=1, keepdims=True) * (1.0 / WIDTH)
    return (v * lax.rsqrt(mean + 1e-06)).astype(jnp.bfloat16)


def norm_all_kernel(x_ref, own_ref, *part_refs):
    i = pl.program_id(0)
    normed = unit_rows(x_ref[...])
    own_ref[...] = normed
    for k, ref in enumerate(part_refs):
        lo, hi = EDGES[k + 1] // STRIP, EDGES[k + 2] // STRIP

        @pl.when((i >= lo) & (i < hi))
        def _(ref=ref):
            ref[...] = normed


def normalize_all(embeddings):
    def part_map(k):
        lo, hi = EDGES[k] // STRIP, EDGES[k + 1] // STRIP
        return lambda i: (jnp.clip(i - lo, 0, hi - lo - 1), 0)

    block = (STRIP, WIDTH)
    later = range(1, len(CHUNKS))
    return pl.pallas_call(
        norm_all_kernel,
        out_shape=[jax.ShapeDtypeStruct((ROWS, WIDTH), jnp.bfloat16)]
        + [jax.ShapeDtypeStruct((CHUNKS[k], WIDTH), jnp.bfloat16) for k in later],
        grid=(ROWS // STRIP,),
        in_specs=[pl.BlockSpec(block, lambda i: (i, 0))],
        out_specs=[pl.BlockSpec(block, lambda i: (i, 0))]
        + [pl.BlockSpec(block, part_map(k)) for k in later],
    )(embeddings)


class Work:
    def __init__(self, info, idr, idc, accr, accc):
        self.info, self.idr, self.idc = info, idr, idc
        self.accr, self.accc = accr, accc
        accr[...] = jnp.zeros_like(accr)
        accc[...] = jnp.zeros_like(accc)
        for s in range(idc.shape[0] // ROWS):
            idc[s * ROWS : (s + 1) * ROWS, :] = jnp.broadcast_to(idr[s], (128, ROWS)).T

    def span(self, slot, first, rows):
        start = self.info[slot * 16 + first // PIECE]
        end = self.info[slot * 16 + 8 + (first + rows) // PIECE - 1]
        return start, end

    def shares(self, a, ra, m, b, cb, n):
        a0, a1 = self.span(a, ra, m)
        b0, b1 = self.span(b, cb, n)
        return (a0 <= b1) & (b0 <= a1)

    def tile(self, left, a, ra, right, b, cb, diagonal=False):
        m, n = left.shape[0], right.shape[0]
        rows = pl.ds(pl.multiple_of(a * ROWS + ra, PIECE), m)
        scores = lax.dot_general(
            left, right, (((1,), (1,)), ((), ())), preferred_element_type=jnp.float32
        )
        ids = self.idc[rows, :]
        best = self.accr[rows, :]
        for g in range(n // 128):
            at = pl.ds(pl.multiple_of(cb + g * 128, 128), 128)
            same = ids == self.idr[b, :, at]
            if diagonal:
                row = lax.broadcasted_iota(jnp.int32, (m, 128), 0) + ra
                col = lax.broadcasted_iota(jnp.int32, (m, 128), 1) + (cb + g * 128)
                same = same & (row != col)
            v = jnp.where(same, scores[:, g * 128 : (g + 1) * 128], 0.0)
            best = jnp.maximum(best, v)
            self.accc[b, :, at] = jnp.maximum(
                self.accc[b, :, at], jnp.max(v.reshape(m // 8, 8, 128), axis=0)
            )
        self.accr[rows, :] = best

    def finish(self, slot, out):
        lanes = self.accr[slot * ROWS : (slot + 1) * ROWS, :]
        best = jnp.max(lanes.T.reshape(128, 8, 128), axis=0)
        cols = jnp.max(self.accc[slot], axis=0, keepdims=True)
        for v in range(8):
            out[slot, v : v + 1, :] = jnp.maximum(
                best[v : v + 1], cols[:, v * 128 : (v + 1) * 128]
            )


def own_kernel(info_ref, own_ref, idr_ref, out_ref, idc, accr, accc):
    work = Work(info_ref, idr_ref, idc, accr, accc)
    size = 512

    def within(i, _):
        ra, cb = lax.div(i, 2) * size, lax.rem(i, 2) * size

        @pl.when(work.shares(0, ra, size, 0, cb, size))
        def _():
            left = own_ref[pl.ds(pl.multiple_of(ra, size), size), :]
            right = own_ref[pl.ds(pl.multiple_of(cb, size), size), :]
            work.tile(left, 0, ra, right, 0, cb, diagonal=True)

        return 0

    lax.fori_loop(0, 4, within, 0)
    work.finish(0, out_ref)


def step_kernel(step, clusters, info_ref, idr_ref, own_ref, sib_ref, *refs):
    last = step == len(CHUNKS) - 1
    new, old, refs = refs[:4], refs[4 : 4 + 4 * step], refs[4 + 4 * step :]
    if last:
        idn_ref, earlier, refs = refs[0], refs[1 : 2 + step], refs[2 + step :]
    out_ref, idc, accr, accc, data, sems = refs[:6]
    found = refs[6] if last else out_ref
    first, size = EDGES[step], CHUNKS[step]
    copies = [
        pltpu.make_async_copy(
            old[s * step + k],
            data.at[pl.ds(s * ROWS + EDGES[k], CHUNKS[k])],
            sems.at[0],
        )
        for s in range(4)
        for k in range(step)
    ]
    for c in copies:
        c.start()
    for s in range(4):
        at = s * ROWS + first
        data[at : at + size, :] = new[s][...]
    work = Work(info_ref, idr_ref, idc, accr, accc)
    table = 16 * SLOTS + SLOTS

    def rows(slot, start, length):
        return data[pl.ds(pl.multiple_of((slot - 2) * ROWS + start, PIECE), length), :]

    def pair(t):
        return info_ref[table + 3 + 2 * t], info_ref[table + 4 + 2 * t]

    def own_tiles(ref, a):
        def body(t, _):
            b = pair(t)[1]

            @pl.when(work.shares(a, 0, ROWS, b, first, size))
            def _():
                work.tile(ref[...], a, 0, rows(b, first, size), b, first)

            return 0

        return body

    def other_tile(t, _):
        a, b = pair(t)
        end = first + size

        @pl.when(work.shares(a, 0, end, b, first, size))
        def _():
            work.tile(rows(a, 0, end), a, 0, rows(b, first, size), b, first)

        if first > 0:

            @pl.when(work.shares(a, first, size, b, 0, first))
            def _():
                work.tile(rows(a, first, size), a, first, rows(b, 0, first), b, 0)

        return 0

    ends = [info_ref[table + i] for i in range(3)]
    lax.fori_loop(0, ends[0], own_tiles(own_ref, 0), 0)
    lax.fori_loop(ends[0], ends[1], own_tiles(sib_ref, 1), 0)
    if step == 0:
        half = ROWS // 2
        core = lax.rem(info_ref[16 * SLOTS], 2)
        for c, (left, right) in enumerate(((own_ref, sib_ref), (sib_ref, own_ref))):

            @pl.when((core == c) & work.shares(c, c * half, half, 1 - c, 0, ROWS))
            def _(c=c, left=left, right=right):
                work.tile(left[c * half : (c + 1) * half, :], c, c * half, right[...], 1 - c, 0)

    for c in copies:
        c.wait()
    lax.fori_loop(ends[1], ends[2], other_tile, 0)
    for s in range(SLOTS):
        work.finish(s, found)
    if not last:
        return

    for s in range(SLOTS):
        best = found[s]
        for ref in earlier[1:]:
            best = jnp.maximum(best, ref[s])
        if s == 0:
            best = jnp.maximum(best, earlier[0][0])
        found[s] = best
    peaks = []
    for c in range(clusters):
        top = jnp.zeros((8, 128), jnp.float32)
        for s in range(SLOTS):
            top = jnp.maximum(top, jnp.where(idn_ref[s] == float(c), found[s], 0.0))
        peaks.append(jnp.max(top, axis=0, keepdims=True))
    peaks.append(jnp.zeros((128 - clusters, 128), jnp.float32))
    peak = jnp.max(jnp.concatenate(peaks, axis=0).T, axis=0, keepdims=True)
    out_ref[:, 0:8, :] = jnp.zeros((out_ref.shape[0], 8, 128), jnp.float32)
    out_ref[:, 8:9, :] = jnp.broadcast_to(peak[None], (out_ref.shape[0], 1, 128))
    for s in range(SLOTS):
        out_ref[info_ref[16 * SLOTS + s], 0:8, :] = found[s]


VMEM = pl.BlockSpec(memory_space=pltpu.VMEM)
SMEM = pl.BlockSpec(memory_space=pltpu.SMEM)
HBM = pl.BlockSpec(memory_space=pl.ANY)
PARAMS = pltpu.CompilerParams(vmem_limit_bytes=30 * 2**20)


def maxima(slots):
    return jax.ShapeDtypeStruct((slots, 8, 128), jnp.float32)


def scratch(slots):
    return [
        pltpu.VMEM((slots * ROWS, 128), jnp.float32),
        pltpu.VMEM((slots * ROWS, 128), jnp.float32),
        pltpu.VMEM((slots, 8, ROWS), jnp.float32),
    ]


def own_maxima(info, own, idr):
    return pl.pallas_call(
        own_kernel,
        out_shape=maxima(1),
        in_specs=[SMEM, VMEM, VMEM],
        out_specs=VMEM,
        scratch_shapes=scratch(1),
        compiler_params=PARAMS,
    )(info, own, idr)


def step_maxima(step, clusters, count, info, idr, own, sibling, new, old, idn, earlier):
    last = step == len(CHUNKS) - 1
    extra = [idn] + earlier if last else []
    out = jax.ShapeDtypeStruct((count, 9, 128), jnp.float32) if last else maxima(SLOTS)
    return pl.pallas_call(
        functools.partial(step_kernel, step, clusters),
        out_shape=out,
        in_specs=[SMEM] + [VMEM] * 7 + [HBM] * len(old) + [VMEM] * len(extra),
        out_specs=VMEM,
        scratch_shapes=scratch(SLOTS)
        + [pltpu.VMEM((4 * ROWS, WIDTH), jnp.bfloat16), pltpu.SemaphoreType.DMA((1,))]
        + ([pltpu.VMEM((SLOTS, 8, 128), jnp.float32)] if last else []),
        compiler_params=PARAMS,
    )(info, idr, own, sibling, *new, *old, *extra)


def local(embeddings, cluster_sizes):
    count = lax.axis_size(AXIS)
    clusters = cluster_sizes.shape[0]
    me = lax.axis_index(AXIS)
    kind = lax.rem(me, RING)
    ring = me - kind

    ends = jnp.cumsum(cluster_sizes)
    blocks = (jnp.asarray(BLOCKS)[kind] + ring) % count
    pos = blocks[:, None] * ROWS + jnp.arange(ROWS, dtype=jnp.int32)[None, :]
    ids = jnp.sum((ends[None, None, :] <= pos[:, :, None]).astype(jnp.int32), axis=2)
    spans = jnp.concatenate([ids[:, ::PIECE], ids[:, PIECE - 1 :: PIECE]], axis=1).reshape(-1)
    info = jnp.concatenate([spans, blocks, jnp.asarray(KIND_TILES)[kind]])
    idr = ids.astype(jnp.float32)[:, None, :]
    idn = ids.astype(jnp.float32).reshape(SLOTS, 8, 128)

    swap = [(i, i ^ 1) for i in range(count)]
    ways = routes(count)

    def send(part):
        return [lax.ppermute(part, AXIS, way) for way in ways]

    steps = len(CHUNKS)
    part = unit_rows(embeddings[: CHUNKS[0]])
    got = [send(part)]
    embeddings, _ = lax.optimization_barrier((embeddings, part))
    own, *parts = normalize_all(embeddings)
    got.append(send(parts[0]))
    sibling = lax.ppermute(own, AXIS, swap)
    earlier = [own_maxima(info, own, idr[:1])]
    for step in range(steps):
        r0, r1, r2 = got[step]
        if step:
            (r0, r1, r2), _ = lax.optimization_barrier(((r0, r1, r2), earlier[-1]))
        passed = jnp.where(kind == 0, r1, jnp.where((kind == 1) | (kind == 7), r2, r0))
        got[step].append(lax.ppermute(passed, AXIS, swap))
        if step + 2 < steps:
            got.append(send(parts[step + 1]))
        if step == 0:
            info, _ = lax.optimization_barrier((info, earlier[0]))
        new = got[step]
        old = [got[k][s] for s in range(4) for k in range(step)]
        result = step_maxima(
            step, clusters, count, info, idr, own, sibling, new, old, idn, earlier
        )
        earlier = earlier + [result]

    back = lax.all_to_all(result, AXIS, 0, 0, tiled=True)
    final = jnp.max(back, axis=0) * (1.0 / WIDTH)
    return final[:8].reshape(ROWS), final[8, :clusters]


def solution(mesh):
    placed = (P(AXIS, None), P())
    return jax.shard_map(
        local, mesh=mesh, in_specs=placed, out_specs=(P(AXIS), P()), check_vma=False
    )
```

```python
import functools

import jax
import jax.numpy as jnp
import numpy as np
from jax import lax
from jax.experimental import pallas as pl
from jax.experimental.pallas import tpu as pltpu
from jax.sharding import PartitionSpec as P

AXIS = "docs"
ROWS = 1024
WIDTH = 1024
RING = 8
SLOTS = 6
PIECE = 128
STRIP = 256
CHUNKS = (512, 512)
EDGES = (0, 512, 1024)

RECEIVED = (
    (3, 6, 9),
    (2, 8, 7),
    (-4, 1, -6),
    (5, -5, 0),
    (6, 10, 11),
    (7, 12, 13),
    (0, -1, 14),
    (1, -3, 4),
)
PASSED = (1, 2, 0, 0, 0, 0, 0, 2)
TILES = (
    ((0, 3), (0, 7), (1, 9), (3, 6), (3, 7), (3, 9), (6, 9), (7, 9)),
    ((0, 8), (1, 8), (2, 6), (2, 7), (2, 8), (6, 8)),
    ((-6, -4), (-6, 1), (-6, 2), (-4, 1), (-4, 2), (-4, 3), (1, 2), (1, 3), (1, 5)),
    ((-5, -4), (-5, 0), (-5, 2), (-5, 3), (-4, 0), (0, 2), (0, 5), (2, 5), (3, 5)),
    ((5, 10), (5, 11), (6, 10), (6, 11), (7, 10), (7, 11)),
    ((4, 6), (4, 12), (5, 6), (5, 7), (5, 13), (6, 12), (6, 13), (7, 13)),
    ((-1, 0), (-1, 4), (-1, 6), (-1, 7), (0, 4), (4, 7), (6, 14)),
    ((-3, 0), (-3, 1), (-3, 4), (0, 6), (1, 4), (1, 6), (1, 7)),
)


def slot_blocks(kind):
    sibling = kind ^ 1
    return (
        (kind, sibling) + RECEIVED[kind] + (RECEIVED[sibling][PASSED[sibling]],)
    )


def tables():
    blocks = np.array([slot_blocks(k) for k in range(RING)], np.int32)
    tiles = np.zeros((RING, 3 + 2 * max(len(v) for v in TILES)), np.int32)
    for k in range(RING):
        held = slot_blocks(k)
        pairs = sorted(tuple(sorted(held.index(v) for v in pair)) for pair in TILES[k])
        assert (0, 1) not in pairs
        tiles[k, :3] = [sum(a < e for a, _ in pairs) for e in (1, 2, SLOTS)]
        tiles[k, 3 : 3 + 2 * len(pairs)] = np.array(pairs).reshape(-1)
    return blocks, tiles


BLOCKS, KIND_TILES = tables()


def check_cover():
    seen = set()
    for k in range(RING):
        for a, b in TILES[k]:
            d = abs(a - b)
            assert d <= RING and {a, b} <= set(slot_blocks(k))
            low = min(a, b) % RING
            assert (low, d) not in seen
            seen.add((low, d))
    for low in range(RING):
        for d in range(1, RING + 1):
            assert ((low, d) in seen) != (d == 1 and low % 2 == 0)


check_cover()


def routes(count):
    out = []
    for slot in range(3):
        route = []
        for i in range(count):
            source = i - i % RING + RECEIVED[i % RING][slot]
            route.append((source % count, i))
        out.append(route)
    return out


def unit_rows(v):
    v = v.astype(jnp.float32)
    square = v * v
    high = square.astype(jnp.bfloat16)
    low = (square - high.astype(jnp.float32)).astype(jnp.bfloat16)
    ones = jnp.ones((WIDTH, 128), jnp.bfloat16)
    total = jnp.dot(high, ones, preferred_element_type=jnp.float32)
    total += jnp.dot(low, ones, preferred_element_type=jnp.float32)
    scale = lax.rsqrt(total * (1.0 / WIDTH) + 1e-06)
    return jnp.concatenate(
        [v[:, g : g + 128] * scale for g in range(0, WIDTH, 128)], axis=1
    ).astype(jnp.bfloat16)


def norm_kernel(x_ref, out_ref):
    out_ref[...] = unit_rows(x_ref[...])


def normalize_first(embeddings):
    block = pl.BlockSpec((STRIP, WIDTH), lambda i: (i, 0))
    return pl.pallas_call(
        norm_kernel,
        out_shape=jax.ShapeDtypeStruct((CHUNKS[0], WIDTH), jnp.bfloat16),
        grid=(CHUNKS[0] // STRIP,),
        in_specs=[block],
        out_specs=block,
    )(embeddings)


def norm_all_kernel(x_ref, own_ref, *part_refs):
    i = pl.program_id(0)
    normed = unit_rows(x_ref[...])
    own_ref[...] = normed
    for k, ref in enumerate(part_refs):
        lo, hi = EDGES[k + 1] // STRIP, EDGES[k + 2] // STRIP

        @pl.when((i >= lo) & (i < hi))
        def _(ref=ref):
            ref[...] = normed


def normalize_all(embeddings):
    def part_map(k):
        lo, hi = EDGES[k] // STRIP, EDGES[k + 1] // STRIP
        return lambda i: (jnp.clip(i - lo, 0, hi - lo - 1), 0)

    block = (STRIP, WIDTH)
    later = range(1, len(CHUNKS))
    return pl.pallas_call(
        norm_all_kernel,
        out_shape=[jax.ShapeDtypeStruct((ROWS, WIDTH), jnp.bfloat16)]
        + [jax.ShapeDtypeStruct((CHUNKS[k], WIDTH), jnp.bfloat16) for k in later],
        grid=(ROWS // STRIP,),
        in_specs=[pl.BlockSpec(block, lambda i: (i, 0))],
        out_specs=[pl.BlockSpec(block, lambda i: (i, 0))]
        + [pl.BlockSpec(block, part_map(k)) for k in later],
    )(embeddings)


class Work:
    def __init__(self, info, idr, idc, accr, accc):
        self.info, self.idr, self.idc = info, idr, idc
        self.accr, self.accc = accr, accc
        accr[...] = jnp.zeros_like(accr)
        accc[...] = jnp.zeros_like(accc)
        for s in range(idc.shape[0] // ROWS):
            idc[s * ROWS : (s + 1) * ROWS, :] = jnp.broadcast_to(idr[s], (128, ROWS)).T

    def span(self, slot, first, rows):
        start = self.info[slot * 16 + first // PIECE]
        end = self.info[slot * 16 + 8 + (first + rows) // PIECE - 1]
        return start, end

    def shares(self, a, ra, m, b, cb, n):
        a0, a1 = self.span(a, ra, m)
        b0, b1 = self.span(b, cb, n)
        return (a0 <= b1) & (b0 <= a1)

    def tile(self, left, a, ra, right, b, cb, diagonal=False):
        m, n = left.shape[0], right.shape[0]
        rows = pl.ds(pl.multiple_of(a * ROWS + ra, PIECE), m)
        scores = lax.dot_general(
            left, right, (((1,), (1,)), ((), ())), preferred_element_type=jnp.float32
        )
        ids = self.idc[rows, :]
        best = self.accr[rows, :]
        for g in range(n // 128):
            at = pl.ds(pl.multiple_of(cb + g * 128, 128), 128)
            same = ids == self.idr[b, :, at]
            if diagonal:
                row = lax.broadcasted_iota(jnp.int32, (m, 128), 0) + ra
                col = lax.broadcasted_iota(jnp.int32, (m, 128), 1) + (cb + g * 128)
                same = same & (row != col)
            v = jnp.where(same, scores[:, g * 128 : (g + 1) * 128], 0.0)
            best = jnp.maximum(best, v)
            self.accc[b, :, at] = jnp.maximum(
                self.accc[b, :, at], jnp.max(v.reshape(m // 8, 8, 128), axis=0)
            )
        self.accr[rows, :] = best

    def finish(self, slot, out):
        cols = jnp.max(self.accc[slot], axis=0, keepdims=True)
        for v in range(8):
            out[slot, v : v + 1, :] = cols[:, v * 128 : (v + 1) * 128]
        if (slot + 1) * ROWS <= self.accr.shape[0]:
            lanes = self.accr[slot * ROWS : (slot + 1) * ROWS, :]
            out[slot] = jnp.maximum(
                out[slot], jnp.max(lanes.T.reshape(128, 8, 128), axis=0)
            )


def own_kernel(info_ref, own_ref, idr_ref, out_ref, idc, accr, accc):
    work = Work(info_ref, idr_ref, idc, accr, accc)
    size = 512

    def within(i, _):
        ra, cb = lax.div(i, 2) * size, lax.rem(i, 2) * size

        @pl.when(work.shares(0, ra, size, 0, cb, size))
        def _():
            left = own_ref[pl.ds(pl.multiple_of(ra, size), size), :]
            right = own_ref[pl.ds(pl.multiple_of(cb, size), size), :]
            work.tile(left, 0, ra, right, 0, cb, diagonal=True)

        return 0

    lax.fori_loop(0, 4, within, 0)
    work.finish(0, out_ref)


def step_kernel(step, clusters, info_ref, idr_ref, own_ref, sib_ref, *refs):
    last = step == len(CHUNKS) - 1
    new, old, refs = refs[:4], refs[4 : 4 + 4 * step], refs[4 + 4 * step :]
    if last:
        idn_ref, earlier, refs = refs[0], refs[1 : 2 + step], refs[2 + step :]
    out_ref, idc, accr, accc, data, sems = refs[:6]
    found = refs[6] if last else out_ref
    first, size = EDGES[step], CHUNKS[step]
    copies = [
        pltpu.make_async_copy(
            old[s * step + k],
            data.at[pl.ds(s * ROWS + EDGES[k], CHUNKS[k])],
            sems.at[0],
        )
        for s in range(4)
        for k in range(step)
    ]
    for c in copies:
        c.start()
    for s in range(4):
        at = s * ROWS + first
        data[at : at + size, :] = new[s][...]
    work = Work(info_ref, idr_ref, idc, accr, accc)
    table = 16 * SLOTS + SLOTS

    def rows(slot, start, length):
        return data[pl.ds(pl.multiple_of((slot - 2) * ROWS + start, PIECE), length), :]

    def pair(t):
        return info_ref[table + 3 + 2 * t], info_ref[table + 4 + 2 * t]

    def own_tiles(ref, a):
        def body(t, _):
            b = pair(t)[1]

            @pl.when(work.shares(a, 0, ROWS, b, first, size))
            def _():
                work.tile(ref[...], a, 0, rows(b, first, size), b, first)

            return 0

        return body

    def other_tile(t, _):
        a, b = pair(t)
        end = first + size

        @pl.when(work.shares(a, 0, end, b, first, size))
        def _():
            work.tile(rows(a, 0, end), a, 0, rows(b, first, size), b, first)

        if first > 0:

            @pl.when(work.shares(a, first, size, b, 0, first))
            def _():
                work.tile(rows(a, first, size), a, first, rows(b, 0, first), b, 0)

        return 0

    ends = [info_ref[table + i] for i in range(3)]
    lax.fori_loop(0, ends[0], own_tiles(own_ref, 0), 0)
    lax.fori_loop(ends[0], ends[1], own_tiles(sib_ref, 1), 0)
    if step == 0:
        half = ROWS // 2
        core = lax.rem(info_ref[16 * SLOTS], 2)
        for c, (left, right) in enumerate(((own_ref, sib_ref), (sib_ref, own_ref))):

            @pl.when((core == c) & work.shares(c, c * half, half, 1 - c, 0, ROWS))
            def _(c=c, left=left, right=right):
                work.tile(left[c * half : (c + 1) * half, :], c, c * half, right[...], 1 - c, 0)

    for c in copies:
        c.wait()
    lax.fori_loop(ends[1], ends[2], other_tile, 0)
    for s in range(SLOTS):
        work.finish(s, found)
    if not last:
        return

    for s in range(SLOTS):
        best = found[s]
        for ref in earlier[1:]:
            best = jnp.maximum(best, ref[s])
        if s == 0:
            best = jnp.maximum(best, earlier[0][0])
        found[s] = best
    peaks = []
    for c in range(clusters):
        top = jnp.zeros((8, 128), jnp.float32)
        for s in range(SLOTS):
            top = jnp.maximum(top, jnp.where(idn_ref[s] == float(c), found[s], 0.0))
        peaks.append(jnp.max(top, axis=0, keepdims=True))
    peaks.append(jnp.zeros((128 - clusters, 128), jnp.float32))
    peak = jnp.max(jnp.concatenate(peaks, axis=0).T, axis=0, keepdims=True)
    out_ref[:, 0:8, :] = jnp.zeros((out_ref.shape[0], 8, 128), jnp.float32)
    out_ref[:, 8:9, :] = jnp.broadcast_to(peak[None], (out_ref.shape[0], 1, 128))
    for s in range(SLOTS):
        out_ref[info_ref[16 * SLOTS + s], 0:8, :] = found[s]


VMEM = pl.BlockSpec(memory_space=pltpu.VMEM)
SMEM = pl.BlockSpec(memory_space=pltpu.SMEM)
HBM = pl.BlockSpec(memory_space=pl.ANY)
PARAMS = pltpu.CompilerParams(vmem_limit_bytes=30 * 2**20)


def maxima(slots):
    return jax.ShapeDtypeStruct((slots, 8, 128), jnp.float32)


def scratch(slots, rows):
    return [
        pltpu.VMEM((rows * ROWS, 128), jnp.float32),
        pltpu.VMEM((rows * ROWS, 128), jnp.float32),
        pltpu.VMEM((slots, 8, ROWS), jnp.float32),
    ]


def own_maxima(info, own, idr):
    return pl.pallas_call(
        own_kernel,
        out_shape=maxima(1),
        in_specs=[SMEM, VMEM, VMEM],
        out_specs=VMEM,
        scratch_shapes=scratch(1, 1),
        compiler_params=PARAMS,
    )(info, own, idr)


def step_maxima(step, clusters, count, info, idr, own, sibling, new, old, idn, earlier):
    last = step == len(CHUNKS) - 1
    extra = [idn] + earlier if last else []
    out = jax.ShapeDtypeStruct((count, 9, 128), jnp.float32) if last else maxima(SLOTS)
    return pl.pallas_call(
        functools.partial(step_kernel, step, clusters),
        out_shape=out,
        in_specs=[SMEM] + [VMEM] * 7 + [HBM] * len(old) + [VMEM] * len(extra),
        out_specs=VMEM,
        scratch_shapes=scratch(SLOTS, SLOTS - 1)
        + [pltpu.VMEM((4 * ROWS, WIDTH), jnp.bfloat16), pltpu.SemaphoreType.DMA((1,))]
        + ([pltpu.VMEM((SLOTS, 8, 128), jnp.float32)] if last else []),
        compiler_params=PARAMS,
    )(info, idr, own, sibling, *new, *old, *extra)


def local(embeddings, cluster_sizes):
    count = lax.axis_size(AXIS)
    clusters = cluster_sizes.shape[0]
    me = lax.axis_index(AXIS)
    kind = lax.rem(me, RING)
    ring = me - kind

    ends = jnp.cumsum(cluster_sizes)
    blocks = (jnp.asarray(BLOCKS)[kind] + ring) % count
    pos = blocks[:, None] * ROWS + jnp.arange(ROWS, dtype=jnp.int32)[None, :]
    ids = jnp.sum((ends[None, None, :] <= pos[:, :, None]).astype(jnp.int32), axis=2)
    spans = jnp.concatenate([ids[:, ::PIECE], ids[:, PIECE - 1 :: PIECE]], axis=1).reshape(-1)
    info = jnp.concatenate([spans, blocks, jnp.asarray(KIND_TILES)[kind]])
    idr = ids.astype(jnp.float32)[:, None, :]
    idn = ids.astype(jnp.float32).reshape(SLOTS, 8, 128)

    swap = [(i, i ^ 1) for i in range(count)]
    ways = routes(count)

    def send(part):
        return [lax.ppermute(part, AXIS, way) for way in ways]

    steps = len(CHUNKS)
    part = normalize_first(embeddings)
    got = [send(part)]
    embeddings, _ = lax.optimization_barrier((embeddings, part))
    own, *parts = normalize_all(embeddings)
    got.append(send(parts[0]))
    sibling = lax.ppermute(own, AXIS, swap)
    earlier = [own_maxima(info, own, idr[:1])]
    for step in range(steps):
        if step:
            got[step], _ = lax.optimization_barrier((got[step], earlier[-1]))
            got[step] = list(got[step])
        choice = jnp.asarray(PASSED, jnp.int32)[kind]
        r0, r1, r2 = got[step]
        passed = jnp.where(choice == 1, r1, jnp.where(choice == 2, r2, r0))
        info, _ = lax.optimization_barrier((info, earlier[-1]))
        got[step].append(lax.ppermute(passed, AXIS, swap))
        if step + 2 < steps:
            got.append(send(parts[step + 1]))
        new = got[step]
        old = [got[k][s] for s in range(4) for k in range(step)]
        result = step_maxima(
            step, clusters, count, info, idr, own, sibling, new, old, idn, earlier
        )
        earlier = earlier + [result]

    back = lax.all_to_all(result, AXIS, 0, 0, tiled=True)
    rows = jnp.max(back[:, :8, :], axis=0) * (1.0 / WIDTH)
    return rows.reshape(ROWS), jnp.max(back[:, 8, :clusters], axis=0) * (1.0 / WIDTH)


def solution(mesh):
    placed = (P(AXIS, None), P())
    return jax.shard_map(
        local, mesh=mesh, in_specs=placed, out_specs=(P(AXIS), P()), check_vma=False
    )
```

```python
import functools

import jax
import jax.numpy as jnp
import numpy as np
from jax import lax
from jax.experimental import pallas as pl
from jax.experimental.pallas import tpu as pltpu
from jax.sharding import PartitionSpec as P

AXIS = "docs"
ROWS = 1024
WIDTH = 1024
RING = 8
SLOTS = 6
PIECE = 128
STRIP = 256
CHUNKS = (512, 512)
EDGES = (0, 512, 1024)

RECEIVED = (
    (3, 6, 9),
    (2, 8, 7),
    (-4, 1, -6),
    (5, -5, 0),
    (6, 10, 11),
    (7, 12, 13),
    (0, -1, 14),
    (1, -3, 4),
)
PASSED = (1, 2, 0, 0, 0, 0, 0, 2)
TILES = (
    ((0, 3), (0, 7), (1, 9), (3, 6), (3, 7), (3, 9), (6, 9), (7, 9)),
    ((0, 8), (1, 8), (2, 6), (2, 7), (2, 8), (6, 8)),
    ((-6, -4), (-6, 1), (-6, 2), (-4, 1), (-4, 2), (-4, 3), (1, 2), (1, 3), (1, 5)),
    ((-5, -4), (-5, 0), (-5, 2), (-5, 3), (-4, 0), (0, 2), (0, 5), (2, 5), (3, 5)),
    ((5, 10), (5, 11), (6, 10), (6, 11), (7, 10), (7, 11)),
    ((4, 6), (4, 12), (5, 6), (5, 7), (5, 13), (6, 12), (6, 13), (7, 13)),
    ((-1, 0), (-1, 4), (-1, 6), (-1, 7), (0, 4), (4, 7), (6, 14)),
    ((-3, 0), (-3, 1), (-3, 4), (0, 6), (1, 4), (1, 6), (1, 7)),
)


def slot_blocks(kind):
    sibling = kind ^ 1
    return (
        (kind, sibling) + RECEIVED[kind] + (RECEIVED[sibling][PASSED[sibling]],)
    )


def tables():
    blocks = np.array([slot_blocks(k) for k in range(RING)], np.int32)
    tiles = np.zeros((RING, 3 + 2 * max(len(v) for v in TILES)), np.int32)
    for k in range(RING):
        held = slot_blocks(k)
        pairs = sorted(tuple(sorted(held.index(v) for v in pair)) for pair in TILES[k])
        assert (0, 1) not in pairs
        tiles[k, :3] = [sum(a < e for a, _ in pairs) for e in (1, 2, SLOTS)]
        tiles[k, 3 : 3 + 2 * len(pairs)] = np.array(pairs).reshape(-1)
    return blocks, tiles


BLOCKS, KIND_TILES = tables()


def check_cover():
    seen = set()
    for k in range(RING):
        for a, b in TILES[k]:
            d = abs(a - b)
            assert d <= RING and {a, b} <= set(slot_blocks(k))
            low = min(a, b) % RING
            assert (low, d) not in seen
            seen.add((low, d))
    for low in range(RING):
        for d in range(1, RING + 1):
            assert ((low, d) in seen) != (d == 1 and low % 2 == 0)


check_cover()


def routes(count):
    out = []
    for slot in range(3):
        route = []
        for i in range(count):
            source = i - i % RING + RECEIVED[i % RING][slot]
            route.append((source % count, i))
        out.append(route)
    return out


def unit_rows(v):
    v = v.astype(jnp.float32)
    square = v * v
    high = square.astype(jnp.bfloat16)
    low = (square - high.astype(jnp.float32)).astype(jnp.bfloat16)
    ones = jnp.ones((WIDTH, 128), jnp.bfloat16)
    total = jnp.dot(high, ones, preferred_element_type=jnp.float32)
    total += jnp.dot(low, ones, preferred_element_type=jnp.float32)
    scale = lax.rsqrt(total * (1.0 / WIDTH) + 1e-06)
    return jnp.concatenate(
        [v[:, g : g + 128] * scale for g in range(0, WIDTH, 128)], axis=1
    ).astype(jnp.bfloat16)


def norm_kernel(x_ref, out_ref):
    out_ref[...] = unit_rows(x_ref[...])


def normalize_first(embeddings):
    block = pl.BlockSpec((STRIP, WIDTH), lambda i: (i, 0))
    return pl.pallas_call(
        norm_kernel,
        out_shape=jax.ShapeDtypeStruct((CHUNKS[0], WIDTH), jnp.bfloat16),
        grid=(CHUNKS[0] // STRIP,),
        in_specs=[block],
        out_specs=block,
    )(embeddings)


def norm_all_kernel(x_ref, own_ref, *part_refs):
    i = pl.program_id(0)
    normed = unit_rows(x_ref[...])
    own_ref[...] = normed
    for k, ref in enumerate(part_refs):
        lo, hi = EDGES[k + 1] // STRIP, EDGES[k + 2] // STRIP

        @pl.when((i >= lo) & (i < hi))
        def _(ref=ref):
            ref[...] = normed


def normalize_all(embeddings):
    def part_map(k):
        lo, hi = EDGES[k] // STRIP, EDGES[k + 1] // STRIP
        return lambda i: (jnp.clip(i - lo, 0, hi - lo - 1), 0)

    block = (STRIP, WIDTH)
    later = range(1, len(CHUNKS))
    return pl.pallas_call(
        norm_all_kernel,
        out_shape=[jax.ShapeDtypeStruct((ROWS, WIDTH), jnp.bfloat16)]
        + [jax.ShapeDtypeStruct((CHUNKS[k], WIDTH), jnp.bfloat16) for k in later],
        grid=(ROWS // STRIP,),
        in_specs=[pl.BlockSpec(block, lambda i: (i, 0))],
        out_specs=[pl.BlockSpec(block, lambda i: (i, 0))]
        + [pl.BlockSpec(block, part_map(k)) for k in later],
    )(embeddings)


class Work:
    def __init__(self, info, idr, idc, accr, accc):
        self.info, self.idr, self.idc = info, idr, idc
        self.accr, self.accc = accr, accc
        accr[...] = jnp.zeros_like(accr)
        accc[...] = jnp.zeros_like(accc)
        for s in range(idc.shape[0] // ROWS):
            idc[s * ROWS : (s + 1) * ROWS, :] = jnp.broadcast_to(idr[s], (128, ROWS)).T

    def span(self, slot, first, rows):
        start = self.info[slot * 16 + first // PIECE]
        end = self.info[slot * 16 + 8 + (first + rows) // PIECE - 1]
        return start, end

    def shares(self, a, ra, m, b, cb, n):
        a0, a1 = self.span(a, ra, m)
        b0, b1 = self.span(b, cb, n)
        return (a0 <= b1) & (b0 <= a1)

    def tile(self, left, a, ra, right, b, cb, diagonal=False):
        m, n = left.shape[0], right.shape[0]
        rows = pl.ds(pl.multiple_of(a * ROWS + ra, PIECE), m)
        scores = lax.dot_general(
            left, right, (((1,), (1,)), ((), ())), preferred_element_type=jnp.float32
        )
        ids = self.idc[rows, :]
        best = self.accr[rows, :]
        for g in range(n // 128):
            at = pl.ds(pl.multiple_of(cb + g * 128, 128), 128)
            same = ids == self.idr[b, :, at]
            if diagonal:
                row = lax.broadcasted_iota(jnp.int32, (m, 128), 0) + ra
                col = lax.broadcasted_iota(jnp.int32, (m, 128), 1) + (cb + g * 128)
                same = same & (row != col)
            v = jnp.where(same, scores[:, g * 128 : (g + 1) * 128], 0.0)
            best = jnp.maximum(best, v)
            self.accc[b, :, at] = jnp.maximum(
                self.accc[b, :, at], jnp.max(v.reshape(m // 8, 8, 128), axis=0)
            )
        self.accr[rows, :] = best

    def finish(self, slot, out):
        cols = jnp.max(self.accc[slot], axis=0, keepdims=True)
        for v in range(8):
            out[slot, v : v + 1, :] = cols[:, v * 128 : (v + 1) * 128]
        if (slot + 1) * ROWS <= self.accr.shape[0]:
            lanes = self.accr[slot * ROWS : (slot + 1) * ROWS, :]
            out[slot] = jnp.maximum(
                out[slot], jnp.max(lanes.T.reshape(128, 8, 128), axis=0)
            )


def own_kernel(info_ref, own_ref, idr_ref, out_ref, idc, accr, accc):
    work = Work(info_ref, idr_ref, idc, accr, accc)
    size = 512

    def within(i, _):
        ra, cb = lax.div(i, 2) * size, lax.rem(i, 2) * size

        @pl.when(work.shares(0, ra, size, 0, cb, size))
        def _():
            left = own_ref[pl.ds(pl.multiple_of(ra, size), size), :]
            right = own_ref[pl.ds(pl.multiple_of(cb, size), size), :]
            work.tile(left, 0, ra, right, 0, cb, diagonal=True)

        return 0

    lax.fori_loop(0, 4, within, 0)
    work.finish(0, out_ref)


def near(step):
    return 3 if step == len(CHUNKS) - 1 else 2


def step_kernel(step, clusters, info_ref, idr_ref, own_ref, sib_ref, *refs):
    last = step == len(CHUNKS) - 1
    new, old, refs = refs[:4], refs[4 : 4 + 4 * step], refs[4 + 4 * step :]
    if last:
        idn_ref, earlier, refs = refs[0], refs[1 : 2 + step], refs[2 + step :]
    out_ref, idc, accr, accc, data, sib, sems = refs[:7]
    found = refs[7] if last else out_ref
    first, size = EDGES[step], CHUNKS[step]
    copies = [
        pltpu.make_async_copy(
            old[s * step + k],
            data.at[pl.ds(s * ROWS + EDGES[k], CHUNKS[k])],
            sems.at[0],
        )
        for s in range(4)
        for k in range(step)
    ]
    newest = [
        pltpu.make_async_copy(new[s], data.at[pl.ds(s * ROWS + first, size)], sems.at[1])
        for s in range(4)
        if s != near(step)
    ]
    beside = pltpu.make_async_copy(sib_ref, sib, sems.at[2])
    for c in newest + [beside] + copies:
        c.start()
    at = near(step) * ROWS + first
    data[at : at + size, :] = new[near(step)][...]
    work = Work(info_ref, idr_ref, idc, accr, accc)
    table = 16 * SLOTS + SLOTS

    def rows(slot, start, length):
        return data[pl.ds(pl.multiple_of((slot - 2) * ROWS + start, PIECE), length), :]

    def pair(t):
        return info_ref[table + 3 + 2 * t], info_ref[table + 4 + 2 * t]

    def own_tiles(ref, a):
        def body(t, _):
            b = pair(t)[1]

            @pl.when(work.shares(a, 0, ROWS, b, first, size))
            def _():
                work.tile(ref[...], a, 0, rows(b, first, size), b, first)

            return 0

        return body

    def other_tile(t, _):
        a, b = pair(t)
        end = first + size

        @pl.when(work.shares(a, 0, end, b, first, size))
        def _():
            work.tile(rows(a, 0, end), a, 0, rows(b, first, size), b, first)

        if first > 0:

            @pl.when(work.shares(a, first, size, b, 0, first))
            def _():
                work.tile(rows(a, first, size), a, first, rows(b, 0, first), b, 0)

        return 0

    ends = [info_ref[table + i] for i in range(3)]
    for c in newest:
        c.wait()
    lax.fori_loop(0, ends[0], own_tiles(own_ref, 0), 0)
    beside.wait()
    lax.fori_loop(ends[0], ends[1], own_tiles(sib, 1), 0)
    if step == 0:
        half = ROWS // 2
        core = lax.rem(info_ref[16 * SLOTS], 2)
        for c, (left, right) in enumerate(((own_ref, sib), (sib, own_ref))):

            @pl.when((core == c) & work.shares(c, c * half, half, 1 - c, 0, ROWS))
            def _(c=c, left=left, right=right):
                work.tile(left[c * half : (c + 1) * half, :], c, c * half, right[...], 1 - c, 0)

    for c in copies:
        c.wait()
    lax.fori_loop(ends[1], ends[2], other_tile, 0)
    for s in range(SLOTS):
        work.finish(s, found)
    if not last:
        return

    for s in range(SLOTS):
        best = found[s]
        for ref in earlier[1:]:
            best = jnp.maximum(best, ref[s])
        if s == 0:
            best = jnp.maximum(best, earlier[0][0])
        found[s] = best
    peaks = []
    for c in range(clusters):
        top = jnp.zeros((8, 128), jnp.float32)
        for s in range(SLOTS):
            top = jnp.maximum(top, jnp.where(idn_ref[s] == float(c), found[s], 0.0))
        peaks.append(jnp.max(top, axis=0, keepdims=True))
    peaks.append(jnp.zeros((128 - clusters, 128), jnp.float32))
    peak = jnp.max(jnp.concatenate(peaks, axis=0).T, axis=0, keepdims=True)
    out_ref[:, 0:8, :] = jnp.zeros((out_ref.shape[0], 8, 128), jnp.float32)
    out_ref[:, 8:9, :] = jnp.broadcast_to(peak[None], (out_ref.shape[0], 1, 128))
    for s in range(SLOTS):
        out_ref[info_ref[16 * SLOTS + s], 0:8, :] = found[s]


VMEM = pl.BlockSpec(memory_space=pltpu.VMEM)
SMEM = pl.BlockSpec(memory_space=pltpu.SMEM)
HBM = pl.BlockSpec(memory_space=pl.ANY)
PARAMS = pltpu.CompilerParams(vmem_limit_bytes=30 * 2**20)


def maxima(slots):
    return jax.ShapeDtypeStruct((slots, 8, 128), jnp.float32)


def scratch(slots, rows):
    return [
        pltpu.VMEM((rows * ROWS, 128), jnp.float32),
        pltpu.VMEM((rows * ROWS, 128), jnp.float32),
        pltpu.VMEM((slots, 8, ROWS), jnp.float32),
    ]


def own_maxima(info, own, idr):
    return pl.pallas_call(
        own_kernel,
        out_shape=maxima(1),
        in_specs=[SMEM, VMEM, VMEM],
        out_specs=VMEM,
        scratch_shapes=scratch(1, 1),
        compiler_params=PARAMS,
    )(info, own, idr)


def step_maxima(step, clusters, count, info, idr, own, sibling, new, old, idn, earlier):
    last = step == len(CHUNKS) - 1
    extra = [idn] + earlier if last else []
    out = jax.ShapeDtypeStruct((count, 9, 128), jnp.float32) if last else maxima(SLOTS)
    return pl.pallas_call(
        functools.partial(step_kernel, step, clusters),
        out_shape=out,
        in_specs=[SMEM, VMEM, VMEM, HBM]
        + [VMEM if s == near(step) else HBM for s in range(4)]
        + [HBM] * len(old) + [VMEM] * len(extra),
        out_specs=VMEM,
        scratch_shapes=scratch(SLOTS, SLOTS - 1)
        + [pltpu.VMEM((4 * ROWS, WIDTH), jnp.bfloat16), pltpu.VMEM((ROWS, WIDTH), jnp.bfloat16), pltpu.SemaphoreType.DMA((3,))]
        + ([pltpu.VMEM((SLOTS, 8, 128), jnp.float32)] if last else []),
        compiler_params=PARAMS,
    )(info, idr, own, sibling, *new, *old, *extra)


def local(embeddings, cluster_sizes):
    count = lax.axis_size(AXIS)
    clusters = cluster_sizes.shape[0]
    me = lax.axis_index(AXIS)
    kind = lax.rem(me, RING)
    ring = me - kind

    ends = jnp.cumsum(cluster_sizes)
    blocks = (jnp.asarray(BLOCKS)[kind] + ring) % count
    pos = blocks[:, None] * ROWS + jnp.arange(ROWS, dtype=jnp.int32)[None, :]
    ids = jnp.sum((ends[None, None, :] <= pos[:, :, None]).astype(jnp.int32), axis=2)
    spans = jnp.concatenate([ids[:, ::PIECE], ids[:, PIECE - 1 :: PIECE]], axis=1).reshape(-1)
    info = jnp.concatenate([spans, blocks, jnp.asarray(KIND_TILES)[kind]])
    idr = ids.astype(jnp.float32)[:, None, :]
    idn = ids.astype(jnp.float32).reshape(SLOTS, 8, 128)

    swap = [(i, i ^ 1) for i in range(count)]
    ways = routes(count)

    def send(part):
        return [lax.ppermute(part, AXIS, way) for way in ways]

    steps = len(CHUNKS)
    part = normalize_first(embeddings)
    got = [send(part)]
    embeddings, _ = lax.optimization_barrier((embeddings, part))
    own, *parts = normalize_all(embeddings)
    got.append(send(parts[0]))
    sibling = lax.ppermute(own, AXIS, swap)
    earlier = [own_maxima(info, own, idr[:1])]
    for step in range(steps):
        if step:
            got[step], _ = lax.optimization_barrier((got[step], earlier[-1]))
            got[step] = list(got[step])
        choice = jnp.asarray(PASSED, jnp.int32)[kind]
        r0, r1, r2 = got[step]
        passed = jnp.where(choice == 1, r1, jnp.where(choice == 2, r2, r0))
        info, _ = lax.optimization_barrier((info, earlier[-1]))
        got[step].append(lax.ppermute(passed, AXIS, swap))
        if step + 2 < steps:
            got.append(send(parts[step + 1]))
        new = got[step]
        old = [got[k][s] for s in range(4) for k in range(step)]
        result = step_maxima(
            step, clusters, count, info, idr, own, sibling, new, old, idn, earlier
        )
        earlier = earlier + [result]

    back = lax.all_to_all(result, AXIS, 0, 0, tiled=True)
    rows = jnp.max(back[:, :8, :], axis=0) * (1.0 / WIDTH)
    return rows.reshape(ROWS), jnp.max(back[:, 8, :clusters], axis=0) * (1.0 / WIDTH)


def solution(mesh):
    placed = (P(AXIS, None), P())
    return jax.shard_map(
        local, mesh=mesh, in_specs=placed, out_specs=(P(AXIS), P()), check_vma=False
    )
```
